32 devices in a mesh: rep: 2 (over core), seq: 4 (over z), shard: 4 (over y, x).
Axes of the slice: x: 2, y: 2, z: 4, core: 2. Of those that a mesh axis runs over, the one named last changes fastest.
Arguments:
- hidden: bfloat16 [16, 2048, 768], P(('rep', 'shard'), 'seq'), may hold values from -6 to 6
- segment: int32 [16, 2048], P(('rep', 'shard')), may hold values from 0 to 127, as said below
- norm_gain: float32 [768], P('shard'), may hold values from 0.5 to 2
- in_weight: float32 [768, 3352], P('shard'), may hold values from -0.21875 to 0.21875
- conv_weight: float32 [4, 1792], P(None, 'shard'), may hold values from -3 to 3
- conv_bias: float32 [1792], P('shard'), may hold values from -3 to 3
- dt_bias: float32 [24], P('shard'), may hold values from -7 to -3
- a_log: float32 [24], P('shard'), may hold values from -1 to 1.5
- skip_d: float32 [24], P('shard'), may hold values from 0.5 to 2
- inner_gain: float32 [1536], P('shard'), may hold values from 0.5 to 2
- out_weight: float32 [1536, 768], P('shard'), may hold values from -0.15625 to 0.15625
- cotangent: bfloat16 [16, 2048, 768], P(('rep', 'shard'), 'seq'), may hold values from -6 to 6
Outputs:
- output: bfloat16 [16, 2048, 768], P(('rep', 'shard'), 'seq')
- hidden_grad: float32 [16, 2048, 768], P(('rep', 'shard'), 'seq')
- norm_gain_grad: float32 [768], P('shard')
- in_weight_grad: float32 [768, 3352], P('shard')
- conv_weight_grad: float32 [4, 1792], P(None, 'shard')
- conv_bias_grad: float32 [1792], P('shard')
- dt_bias_grad: float32 [24], P('shard')
- a_log_grad: float32 [24], P('shard')
- skip_d_grad: float32 [24], P('shard')
- inner_gain_grad: float32 [1536], P('shard')
- out_weight_grad: float32 [1536, 768], P('shard')
The draws below stay inside these ranges and needn't reach their ends.
Inputs may be any that keep to these rules, and one draw needn't show every extreme that they name: `segment`: along each row the document numbers never fall and rise by at most one from one position to the next; the first position has number 0; some row reaches the largest number.
All inputs are finite; a program needn't handle non-finite values.
Results may differ from the reference program's by a relative error of at most 0.0018.
The reference program's roundings to bfloat16 on the way count: a program that leaves them out, or rounds other values in their place, can miss the bound.
Values may be sent and summed in bfloat16 or wider, within the bound.
No kernel may reach another device: no remote copies, remote signals or barrier semaphores. Data moves between devices by JAX's collectives and lax.ppermute only.
A program may use at most 256 MiB of HBM per device.

```python
import math
import jax
import jax.numpy as jnp
from jax import lax

D = 768
HEADS = 24
HEAD_DIM = 64
STATE = 128
WIDTH = 4
SPAN = 256
SEQ_GRP = 2
PIECE = 512
INNER = 1536
CONV_CH = 1792
PROJ = 3352
LEN = 2048
SEQS = 16


def draw_segment(key, part):
    key = jax.random.fold_in(key, 11)
    key_rate, key_roll, key_pick, key_start, key_stop = jax.random.split(key, 5)
    rate_level = jax.random.randint(key_rate, (SEQS, 1), 0, 3)
    period = 16 * jnp.power(4, rate_level)
    rolled = jax.random.randint(key_roll, (SEQS, LEN), 0, 1 << 20)
    flags = rolled % period == 0
    chosen = jax.random.randint(key_pick, (SEQS // SEQ_GRP, 1), 0, SEQ_GRP)
    row_index = jnp.arange(SEQS)[:, None]
    is_long = row_index % SEQ_GRP == jnp.repeat(chosen, SEQ_GRP, axis=0)
    begin_at = jax.random.randint(key_start, (SEQS, 1), 0, PIECE // 2)
    end_at = LEN - jax.random.randint(key_stop, (SEQS, 1), 0, PIECE // 2)
    position = jnp.arange(LEN)[None, :]
    inside = (position > begin_at) & (position < end_at)
    flags = jnp.where(is_long & inside, False, flags)
    flags = flags | is_long & ((position == begin_at) | (position == end_at))
    forced_row = (chosen[0, 0] + 1) % SEQ_GRP
    flags = flags | (row_index == forced_row) & (position % 16 == 0)
    flags = flags | (position == 0)
    numbers = jnp.cumsum(flags.astype(jnp.int32), axis=1) - 1
    return jnp.minimum(numbers, LEN // 16 - 1).astype(jnp.int32)


def steps_of(stream_key, shape, cuts, least, largest):
    level, own = 1.0, jax.random.fold_in(stream_key, 6)
    for dim, blocks in cuts:
        steps = jnp.exp(jax.random.uniform(jax.random.fold_in(own, dim), (blocks,), jnp.float32, least / len(cuts), largest / len(cuts)))
        level = level * jnp.repeat(steps, shape[dim] // blocks).reshape([-1 if axis == dim else 1 for axis in range(len(shape))])
    return level


def noise(rng, dims, scale, most, cuts=(), kind=jnp.bfloat16):
    values = scale * jax.random.normal(rng, dims, jnp.float32)
    if cuts:
        values = values * steps_of(rng, dims, cuts, -0.22, 0.18)
    return jnp.clip(values, -most, most).astype(kind)


def setup_inputs(seed: int = 0) -> dict:
    key_list = jax.random.split(jax.random.key(seed), 13)
    hidden = noise(key_list[0], (SEQS, LEN, D), 1.0, 6.0, ((0, 8), (1, 4)))
    segment = draw_segment(jax.random.fold_in(key_list[12], 71), 0)
    norm_gain = jnp.clip(jnp.exp(math.log(2.0) - 1.3862944 * jax.random.uniform(key_list[2], (D,), jnp.float32) ** steps_of(key_list[2], (D,), ((0, 4),), -0.2, 0.2)), 0.5, 2.0)
    in_weight = noise(key_list[3], (D, PROJ), D ** -0.5, 0.21875, ((0, 4),), jnp.float32)
    conv_weight = noise(key_list[4], (WIDTH, CONV_CH), WIDTH ** -0.5, 3.0, ((1, 4),), jnp.float32)
    conv_bias = noise(key_list[5], (CONV_CH,), 0.5, 3.0, ((0, 4),), jnp.float32)
    dt_bias = jnp.clip(-7.0 + 4.0 * jax.random.uniform(key_list[6], (HEADS,), jnp.float32) ** steps_of(key_list[6], (HEADS,), ((0, 4),), -0.2, 0.2), -7.0, -3.0)
    a_log = jnp.clip(-1.0 + 2.5 * jax.random.uniform(key_list[7], (HEADS,), jnp.float32) ** steps_of(key_list[7], (HEADS,), ((0, 4),), -0.2, 0.2), -1.0, 1.5)
    skip_d = jnp.clip(0.5 + 1.5 * jax.random.uniform(key_list[8], (HEADS,), jnp.float32) ** steps_of(key_list[8], (HEADS,), ((0, 4),), -0.2, 0.2), 0.5, 2.0)
    inner_gain = jnp.clip(jnp.exp(math.log(2.0) - 1.3862944 * jax.random.uniform(key_list[9], (INNER,), jnp.float32) ** steps_of(key_list[9], (INNER,), ((0, 4),), -0.2, 0.2)), 0.5, 2.0)
    out_weight = noise(key_list[10], (INNER, D), INNER ** -0.5, 0.15625, ((0, 4),), jnp.float32)
    cotangent = noise(key_list[11], (SEQS, LEN, D), 1.0, 6.0, ((0, 8), (1, 4)))
    return {"hidden": hidden, "segment": segment, "norm_gain": norm_gain, "in_weight": in_weight, "conv_weight": conv_weight, "conv_bias": conv_bias, "dt_bias": dt_bias, "a_log": a_log, "skip_d": skip_d, "inner_gain": inner_gain, "out_weight": out_weight, "cotangent": cotangent}


norm_epsilon = 1e-05
exact_mode = lax.Precision.HIGHEST

@jax.custom_vjp
def low(v):
    return lax.optimization_barrier(v.astype(jnp.bfloat16)).astype(jnp.float32)

@jax.custom_vjp
def low_back(v):
    return v

def low_keep(v):
    return (low(v), None)

def low_pass(kept, grad):
    return (grad,)

def back_keep(v):
    return (v, None)

def back_low(kept, grad):
    return (low(grad),)
low.defvjp(low_keep, low_pass)
low_back.defvjp(back_keep, back_low)

def span_step(state_in, pieces):
    head_x, b_mat, c_mat, decay_log, step_size, seg_blk, prev_seg = pieces
    width_q = seg_blk.shape[1]
    cum_log = jnp.cumsum(decay_log, axis=1)
    causal = jnp.arange(width_q)[:, None] >= jnp.arange(width_q)[None, :]
    joined = (seg_blk[:, :, None] == seg_blk[:, None, :]) & causal[None]
    spread = cum_log[:, :, None, :] - cum_log[:, None, :, :]
    weights = jnp.where(joined[..., None], jnp.exp(jnp.where(joined[..., None], spread, 0.0)), 0.0)
    inner_prod = jnp.einsum('btn,bsn->bts', c_mat, b_mat, precision=exact_mode)
    mixing = inner_prod[..., None] * weights * step_size[:, None, :, :]
    within = jnp.einsum('btsh,bshp->bthp', mixing, head_x, precision=exact_mode)
    keep_mask = (seg_blk == prev_seg[:, None]).astype(jnp.float32)
    carried = jnp.einsum('btn,bhpn->bthp', c_mat, state_in, precision=exact_mode)
    carried = carried * (keep_mask[:, :, None] * jnp.exp(cum_log))[..., None]
    last_seg = seg_blk[:, -1]
    tail_mask = (seg_blk == last_seg[:, None]).astype(jnp.float32)
    scale_w = tail_mask[:, :, None] * jnp.exp(cum_log[:, -1:, :] - cum_log) * step_size
    fresh_state = jnp.einsum('bshp,bsn->bhpn', head_x * scale_w[..., None], b_mat, precision=exact_mode)
    through = (last_seg == prev_seg).astype(jnp.float32)[:, None] * jnp.exp(cum_log[:, -1, :])
    return (through[:, :, None, None] * state_in + fresh_state, within + carried)

def ssd_blocks(head_x, b_mat, c_mat, decay_log, step_size, seg_ext, length):
    row_count = head_x.shape[0]
    blocks = length // SPAN

    def to_blocks(array):
        return jnp.moveaxis(array.reshape((row_count, blocks, SPAN) + array.shape[2:]), 1, 0)
    prev_seg = jnp.moveaxis(seg_ext[:, WIDTH - 2:WIDTH - 2 + length:SPAN], 1, 0)
    seg_blk = to_blocks(seg_ext[:, WIDTH - 1:])
    zero_state = jnp.zeros((row_count, HEADS, HEAD_DIM, STATE), jnp.float32)
    final_state, outputs = lax.scan(jax.checkpoint(span_step), zero_state, (to_blocks(head_x), to_blocks(b_mat), to_blocks(c_mat), to_blocks(decay_log), to_blocks(step_size), seg_blk, prev_seg))
    return (final_state, jnp.moveaxis(outputs, 0, 1).reshape(row_count, length, HEADS, HEAD_DIM))

def conv_mix(conv_ext, seg_ext, weight_conv, bias_conv, length):
    seg_own = seg_ext[:, WIDTH - 1:]
    summed = bias_conv
    for shift_back in range(WIDTH):
        first_row = WIDTH - 1 - shift_back
        valid_mask = (seg_ext[:, first_row:first_row + length] == seg_own).astype(jnp.float32)
        summed = summed + weight_conv[WIDTH - 1 - shift_back] * conv_ext[:, first_row:first_row + length, :] * valid_mask[:, :, None]
    return jax.nn.silu(summed)

def mix_core(activated, dt_raw, bias_dt, log_a, seg_ext, length):
    row_count = activated.shape[0]
    head_x = activated[:, :, :INNER].reshape(row_count, length, HEADS, HEAD_DIM)
    b_mat = activated[:, :, INNER:INNER + STATE]
    c_mat = activated[:, :, INNER + STATE:]
    step_size = jax.nn.softplus(dt_raw + bias_dt)
    decay_log = -jnp.exp(log_a) * step_size
    final_state, ssd = ssd_blocks(head_x, b_mat, c_mat, decay_log, step_size, seg_ext, length)
    return (final_state, ssd, head_x, c_mat, decay_log)

def gate_norm(ssd, head_x, gate_z, skip_v, gain_i):
    row_count, length = (gate_z.shape[0], gate_z.shape[1])
    y_full = (ssd + skip_v[:, None] * head_x).reshape(row_count, length, INNER)
    gated = y_full * jax.nn.silu(gate_z)
    return gated * lax.rsqrt(lax.optimization_barrier(jnp.mean(gated * gated, axis=-1, keepdims=True)) + norm_epsilon) * gain_i

def layer_forward(hidden_f, seg_rows, norm_gain, in_weight, conv_weight, conv_bias, dt_bias, a_log, skip_d, inner_gain, out_weight):
    row_count, length = seg_rows.shape
    gain_n = low(norm_gain)
    weight_in = low(in_weight)
    weight_conv = low(conv_weight)
    bias_conv = low(conv_bias)
    bias_dt = low(dt_bias)
    log_a = low(a_log)
    skip_v = low(skip_d)
    gain_i = low(inner_gain)
    weight_out = low(out_weight)
    mean_sq = lax.optimization_barrier(jnp.mean(hidden_f * hidden_f, axis=-1, keepdims=True))
    normed = low(hidden_f * lax.rsqrt(mean_sq + norm_epsilon) * gain_n)
    proj = jnp.einsum('btd,de->bte', normed, weight_in, precision=exact_mode)
    proj = low_back(low(proj))
    gate_z = proj[:, :, :INNER]
    conv_in = proj[:, :, INNER:INNER + CONV_CH]
    dt_raw = proj[:, :, INNER + CONV_CH:]
    seg_ext = jnp.concatenate([jnp.full((row_count, WIDTH - 1), -1, jnp.int32), seg_rows.astype(jnp.int32)], axis=1)
    conv_ext = jnp.concatenate([jnp.zeros((row_count, WIDTH - 1, CONV_CH), jnp.float32), conv_in], axis=1)
    activated = conv_mix(conv_ext, seg_ext, weight_conv, bias_conv, length)
    final_state, ssd, head_x, c_mat, decay_log = mix_core(activated, dt_raw, bias_dt, log_a, seg_ext, length)
    ssd = low_back(ssd)
    out_norm = low(gate_norm(ssd, head_x, gate_z, skip_v, gain_i))
    branch = jnp.einsum('bti,id->btd', out_norm, weight_out, precision=exact_mode)
    return hidden_f + branch

def reference(hidden, segment, norm_gain, in_weight, conv_weight, conv_bias, dt_bias, a_log, skip_d, inner_gain, out_weight, cotangent):
    groups = SEQS // SEQ_GRP
    params = (norm_gain, in_weight, conv_weight, conv_bias, dt_bias, a_log, skip_d, inner_gain, out_weight)
    hidden_g = hidden.astype(jnp.float32).reshape(groups, SEQ_GRP, LEN, D)
    seg_g = segment.reshape(groups, SEQ_GRP, LEN)
    cot_g = cotangent.astype(jnp.float32).reshape(groups, SEQ_GRP, LEN, D)

    def group_step(totals, pieces):
        hid_v, seg_v, cot_v = pieces

        def apply_layer(hid_in, *weights):
            return layer_forward(hid_in, seg_v, *weights)
        result, pull_back = jax.vjp(apply_layer, hid_v, *params)
        grads = pull_back(cot_v)
        new_totals = tuple((total + grad for total, grad in zip(totals, grads[1:])))
        return (new_totals, (result.astype(jnp.bfloat16), grads[0]))
    zeros_init = tuple((jnp.zeros_like(param) for param in params))
    totals, (results, hidden_grads) = lax.scan(group_step, zeros_init, (hidden_g, seg_g, cot_g))
    return (results.reshape(SEQS, LEN, D), hidden_grads.reshape(SEQS, LEN, D), totals[0], totals[1], totals[2], totals[3], totals[4], totals[5], totals[6], totals[7], totals[8])
```

```python
import functools

import jax
import jax.numpy as jnp
from jax import lax
from jax.experimental import pallas as pl
from jax.experimental.pallas import tpu as pltpu
from jax.sharding import PartitionSpec as P

D = 768
HEADS = 24
HEAD_DIM = 64
STATE = 128
WIDTH = 4
INNER = 1536
CONV_CH = 1792
PROJ = 3352
MIX = PROJ - INNER
Q = 128
GRP = 256
LANES = 128
PAIRS = HEADS // 2
EDGE = 16

norm_epsilon = 1e-05
F32 = jnp.float32
BF = jnp.bfloat16
VMEM_LIMIT = 40 * 1024 * 1024


def split2(value):
    high = value.astype(BF)
    return high, (value - high.astype(F32)).astype(BF)


def split3(value):
    high = value.astype(BF)
    rest = value - high.astype(F32)
    mid = rest.astype(BF)
    return high, mid, (rest - mid.astype(F32)).astype(BF)


def mm(left, right):
    return jnp.dot(left, right, preferred_element_type=F32)


def mm_nt(left, right):
    return lax.dot_general(left, right, (((1,), (1,)), ((), ())), preferred_element_type=F32)


def mm3(left, right):
    lh, ll = split2(left)
    rh, rl = split2(right)
    return mm(lh, rh) + mm(lh, rl) + mm(ll, rh)


def mm3_nt(left, right):
    lh, ll = split2(left)
    rh, rl = split2(right)
    return mm_nt(lh, rh) + mm_nt(lh, rl) + mm_nt(ll, rh)


def stacked_left(left):
    lh, ll = split2(left)
    return jnp.concatenate([lh, lh], axis=1), ll


def mm3_stacked(left_pair, right):
    both, low_part = left_pair
    rh, rl = split2(right)
    return mm(both, jnp.concatenate([rh, rl], axis=0)) + mm(low_part, rh)


def spread_heads(parts, table):
    return mm(parts[0], table) + mm(parts[1], table)


def sigmoid(value):
    return 0.5 * jnp.tanh(0.5 * value) + 0.5


def pair_rows(pair):
    lane = lax.broadcasted_iota(jnp.int32, pair.shape, 1)
    zero = jnp.zeros_like(pair)
    first = jnp.where(lane < HEAD_DIM, pair, zero)
    second = jnp.where(lane >= HEAD_DIM, pair, zero)
    return jnp.concatenate([first, second], axis=0)


def lanes_of(group):
    return slice(group * GRP, (group + 1) * GRP)


def front_kernel(
    cur_ref,
    prev_ref,
    rim_ref,
    cols_ref,
    taps_ref,
    bias_ref,
    bias_dt_ref,
    neg_a_ref,
    table_ref,
    tri_ref,
    u_ref,
    xh_ref,
    xl_ref,
    bc_ref,
    step_ref,
    cum_ref,
    sig_ref,
    cum_t_ref,
    start_ref,
    final_ref,
    reach_ref,
    whole_ref,
    ext,
    state,
    reach,
):
    chunk = pl.program_id(1)
    chunks = pl.num_programs(1)

    @pl.when(chunk == 0)
    def _():
        state[...] = jnp.zeros_like(state)
        reach[...] = jnp.ones_like(reach)
        ext[0:EDGE, :] = rim_ref[0, :, :CONV_CH].astype(F32)

    @pl.when(chunk > 0)
    def _():
        ext[0:EDGE, :] = prev_ref[0, :, :CONV_CH].astype(F32)

    ext[EDGE : EDGE + Q, :] = cur_ref[0, :, :CONV_CH].astype(F32)
    cols = cols_ref[0]
    keep, tail = cols[:, 3:4], cols[:, 4:5]
    shifted_dt = cur_ref[0, :, CONV_CH:MIX].astype(F32) + bias_dt_ref[...]
    small = jnp.exp(-jnp.abs(shifted_dt))
    ratio = small / (2.0 + small)
    square = ratio * ratio
    series = 1.0 / 15.0
    for odd in (13.0, 11.0, 9.0, 7.0, 5.0, 3.0, 1.0):
        series = series * square + 1.0 / odd
    step = jnp.maximum(shifted_dt, 0.0) + 2.0 * ratio * series
    sig_ref[0] = jnp.where(shifted_dt >= 0.0, 1.0, small) / (1.0 + small)
    decay = neg_a_ref[...] * step
    cum = sum(mm(tri_ref[...], part) for part in split3(decay))
    step_ref[0] = step
    cum_ref[0] = cum
    padded = jnp.concatenate([cum, jnp.zeros((Q, LANES - HEADS), F32)], axis=1)
    cum_t_ref[0] = padded.T[:HEADS, :]
    last = cum[Q - 1 : Q, :]
    tail_w = tail * jnp.exp(last - cum) * step
    through = keep[Q - 1 : Q, :] * jnp.exp(last)
    table = table_ref[...]
    through_row = spread_heads(split2(jnp.broadcast_to(through, (8, HEADS))), table)
    step_parts = split2(step)
    tail_parts = split2(tail_w)

    def conv_act(lanes):
        summed = bias_ref[:, lanes] + taps_ref[3:4, lanes] * ext[EDGE : EDGE + Q, lanes]
        for back in (1, 2, 3):
            summed = summed + taps_ref[3 - back : 4 - back, lanes] * (
                ext[EDGE - back : EDGE - back + Q, lanes] * cols[:, back - 1 : back]
            )
        u_ref[0, :, lanes] = summed
        return summed * sigmoid(summed)

    b_and_c = conv_act(slice(INNER, CONV_CH))
    bc_ref[0] = b_and_c
    b_t = stacked_left(b_and_c[:, :STATE].T)
    start_ref[0, 0] = state[...]
    for group in range(INNER // GRP):
        lanes = lanes_of(group)
        act = conv_act(lanes)
        xh, xl = split2(act * spread_heads(step_parts, table[:, lanes]))
        xh_ref[0, :, lanes] = xh
        xl_ref[0, :, lanes] = xl
        fresh = mm3_stacked(b_t, act * spread_heads(tail_parts, table[:, lanes]))
        state[:, lanes] = through_row[0:1, lanes] * state[:, lanes] + fresh
    reach_ref[0, 0] = reach[...]
    reach[...] = reach[...] * through_row

    @pl.when(chunk == chunks - 1)
    def _():
        final_ref[0] = state[...]
        whole_ref[0] = reach[...]


def within_kernel(bc_ref, cum_ref, cum_t_ref, cols_ref, seg_ref, xh_ref, xl_ref, y_ref):
    b_mat, c_mat = bc_ref[0, :, :STATE], bc_ref[0, :, STATE:]
    rows = lax.broadcasted_iota(jnp.int32, (Q, Q), 0)
    lanes = lax.broadcasted_iota(jnp.int32, (Q, Q), 1)
    joined = (cols_ref[0, :, 5:6] == seg_ref[0]) & (rows >= lanes)
    inner = jnp.where(joined, mm3_nt(c_mat, b_mat), 0.0)
    cum, cum_t = cum_ref[0], cum_t_ref[0]
    for pair in range(PAIRS):
        at = slice(pair * LANES, (pair + 1) * LANES)
        halves = []
        for head in (2 * pair, 2 * pair + 1):
            gap = jnp.minimum(cum[:, head : head + 1] - cum_t[head : head + 1, :], 0.0)
            halves.append(inner * jnp.exp(gap))
        mh, ml = split2(jnp.concatenate(halves, axis=1))
        right_h, right_l = pair_rows(xh_ref[0, :, at]), pair_rows(xl_ref[0, :, at])
        y_ref[0, :, at] = mm(mh, right_h) + mm(mh, right_l) + mm(ml, right_h)


def gate_kernel(
    y_ref,
    u_ref,
    z_ref,
    dgn_ref,
    bc_ref,
    cum_ref,
    cols_ref,
    start_ref,
    reach_ref,
    inc_ref,
    skip_ref,
    gain_ref,
    table_ref,
    fold_ref,
    gnorm_ref,
    dz_ref,
    dyh_ref,
    dyl_ref,
    ry_ref,
    dc_ref,
    dend_ref,
    dstart_ref,
    after_ref,
    dskip_ref,
    dgain_ref,
    y_all,
    full_all,
    w_all,
    d_state,
    after,
):
    row, back = pl.program_id(0), pl.program_id(1)
    chunks = pl.num_programs(1)

    @pl.when(back == 0)
    def _():
        d_state[...] = jnp.zeros_like(d_state)
        after[...] = jnp.ones_like(after)

    @pl.when((back == 0) & (row == 0))
    def _():
        dskip_ref[...] = jnp.zeros_like(dskip_ref)
        dgain_ref[...] = jnp.zeros_like(dgain_ref)

    c_mat = bc_ref[0]
    c_pair = stacked_left(c_mat)
    c_t = stacked_left(c_mat.T)
    cum = cum_ref[0]
    weight = cols_ref[0, :, 3:4] * jnp.exp(cum)
    w_parts = split2(weight)
    table = table_ref[...]
    through = jnp.broadcast_to(weight[Q - 1 : Q, :], (8, HEADS))
    through_row = spread_heads(split2(through), table)
    squares = jnp.zeros((Q, GRP), F32)
    dots = jnp.zeros((Q, GRP), F32)
    for group in range(INNER // GRP):
        lanes = lanes_of(group)
        start = start_ref[0, 0, :, lanes] + reach_ref[0, 0, 0:1, lanes] * inc_ref[
            0, :, lanes
        ].astype(F32)
        w_wide = spread_heads(w_parts, table[:, lanes])
        w_all[:, lanes] = w_wide
        y = y_ref[0, :, lanes] + w_wide * mm3_stacked(c_pair, start)
        y_all[:, lanes] = y
        u = u_ref[0, :, lanes]
        full = y + skip_ref[:, lanes] * (u * sigmoid(u))
        full_all[:, lanes] = full
        z = z_ref[0, :, lanes].astype(F32)
        gated = full * (z * sigmoid(z))
        squares = squares + gated * gated
        dots = dots + gated * (dgn_ref[0, :, lanes] * gain_ref[:, lanes])
    inverse = lax.rsqrt(jnp.sum(squares, axis=1, keepdims=True) * (1.0 / INNER) + norm_epsilon)
    pull = jnp.sum(dots, axis=1, keepdims=True) * (1.0 / INNER) * inverse * inverse * inverse
    row_y = jnp.zeros((Q, LANES), F32)
    d_c = jnp.zeros((Q, STATE), F32)
    dend_ref[0, 0] = d_state[...]
    for group in range(INNER // GRP):
        lanes = lanes_of(group)
        z = z_ref[0, :, lanes].astype(F32)
        sig = sigmoid(z)
        silu = z * sig
        full = full_all[:, lanes]
        gated = full * silu
        dgn = dgn_ref[0, :, lanes]
        unit = gated * inverse
        gain = gain_ref[:, lanes]
        gnorm_ref[0, :, lanes] = (unit * gain).astype(BF)
        dgain_ref[:, lanes] += jnp.sum((dgn * unit).reshape(Q // 8, 8, GRP), axis=0)
        d_gated = dgn * gain * inverse - gated * pull
        dz_ref[0, :, lanes] = (d_gated * full * (sig + silu * (1.0 - sig))).astype(BF)
        dy = d_gated * silu
        u = u_ref[0, :, lanes]
        dskip_ref[:, lanes] += jnp.sum((dy * (u * sigmoid(u))).reshape(Q // 8, 8, GRP), axis=0)
        dyh, dyl = split2(dy)
        dyh_ref[0, :, lanes] = dyh
        dyl_ref[0, :, lanes] = dyl
        dyf = dyh.astype(F32)
        ph, plow = split2(dyf * y_all[:, lanes])
        row_y = row_y + mm(ph, fold_ref[lanes, :]) + mm(plow, fold_ref[lanes, :])
        weighted = w_all[:, lanes] * dyf
        start = start_ref[0, 0, :, lanes] + reach_ref[0, 0, 0:1, lanes] * inc_ref[
            0, :, lanes
        ].astype(F32)
        d_c = d_c + mm3_nt(weighted, start)
        d_state[:, lanes] = through_row[0:1, lanes] * d_state[:, lanes] + mm3_stacked(
            c_t, weighted
        )
    ry_ref[0] = row_y
    dc_ref[0] = d_c
    after_ref[0, 0] = after[...]
    after[...] = after[...] * through_row

    @pl.when(back == chunks - 1)
    def _():
        dstart_ref[0] = d_state[...]


def within_back_kernel(
    bc_ref, cum_ref, cum_t_ref, cols_ref, seg_ref, xh_ref, xl_ref, dyh_ref, dx_ref, dbc_ref
):
    b_mat, c_mat = bc_ref[0, :, :STATE], bc_ref[0, :, STATE:]
    rows = lax.broadcasted_iota(jnp.int32, (Q, Q), 0)
    lanes = lax.broadcasted_iota(jnp.int32, (Q, Q), 1)
    joined = (cols_ref[0, :, 5:6] == seg_ref[0]) & (lanes >= rows)
    inner = jnp.where(joined, mm3_nt(b_mat, c_mat), 0.0)
    cum, cum_t = cum_ref[0], cum_t_ref[0]
    d_inner = jnp.zeros((Q, Q), F32)
    for pair in range(PAIRS):
        at = slice(pair * LANES, (pair + 1) * LANES)
        dy_rows = pair_rows(dyh_ref[0, :, at])
        d_mix = mm_nt(xh_ref[0, :, at], dy_rows) + mm_nt(xl_ref[0, :, at], dy_rows)
        halves = []
        for half, head in enumerate((2 * pair, 2 * pair + 1)):
            gap = jnp.minimum(cum_t[head : head + 1, :] - cum[:, head : head + 1], 0.0)
            factor = jnp.exp(gap)
            d_inner = d_inner + d_mix[:, half * Q : (half + 1) * Q] * factor
            halves.append(inner * factor)
        mh, ml = split2(jnp.concatenate(halves, axis=1))
        dx_ref[0, :, at] = mm(mh, dy_rows) + mm(ml, dy_rows)
    d_inner = jnp.where(joined, d_inner, 0.0)
    dbc_ref[0, :, :STATE] = mm3(d_inner, c_mat)
    dbc_ref[0, :, STATE:] = mm3(d_inner.T, b_mat)


def back_kernel(
    dx_ref,
    dbc_ref,
    dc_ref,
    u_ref,
    xh_ref,
    xl_ref,
    dyh_ref,
    dyl_ref,
    ry_ref,
    step_ref,
    cum_ref,
    sig_ref,
    cols_ref,
    edge_cols_ref,
    bc_ref,
    dend_ref,
    after_ref,
    pass_ref,
    final_ref,
    whole_ref,
    inc_ref,
    cur_ref,
    prev_ref,
    rim_ref,
    taps_ref,
    skip_ref,
    neg_a_ref,
    table_ref,
    fold_ref,
    tri_ref,
    dproj_ref,
    edge_ref,
    rim_grad_ref,
    dtaps_ref,
    dbias_ref,
    dsmall_ref,
    ext,
    du_ext,
    energy,
):
    row, back = pl.program_id(0), pl.program_id(1)
    chunks = pl.num_programs(1)
    table = table_ref[...]

    @pl.when(back == 0)
    def _():
        du_ext[EDGE // 2 + Q :, :] = jnp.zeros((EDGE // 2, CONV_CH), F32)
        du_ext[: EDGE // 2, :] = jnp.zeros((EDGE // 2, CONV_CH), F32)
        total = jnp.zeros((8, LANES), F32)
        for group in range(INNER // GRP):
            lanes = lanes_of(group)
            ends = final_ref[0, :, lanes] + whole_ref[0, 0:1, lanes] * inc_ref[
                0, :, lanes
            ].astype(F32)
            product = ends * pass_ref[0, :, lanes].astype(F32)
            folded = jnp.sum(product.reshape(STATE // 8, 8, GRP), axis=0)
            for part in split3(folded):
                total = total + mm(part, fold_ref[lanes, :])
        energy[...] = jnp.broadcast_to(jnp.sum(total, axis=0, keepdims=True), (8, LANES))

    @pl.when(back > 0)
    def _():
        du_ext[EDGE // 2 + Q :, :] = du_ext[EDGE // 2 : EDGE, :]

    @pl.when((back == 0) & (row == 0))
    def _():
        dtaps_ref[...] = jnp.zeros_like(dtaps_ref)
        dbias_ref[...] = jnp.zeros_like(dbias_ref)
        dsmall_ref[...] = jnp.zeros_like(dsmall_ref)

    @pl.when(back == chunks - 1)
    def _():
        ext[0:EDGE, :] = rim_ref[0, :, :CONV_CH].astype(F32)

    @pl.when(back < chunks - 1)
    def _():
        ext[0:EDGE, :] = prev_ref[0, :, :CONV_CH].astype(F32)

    ext[EDGE : EDGE + Q, :] = cur_ref[0, :, :CONV_CH].astype(F32)
    cols = cols_ref[0]
    step = step_ref[0]
    cum = cum_ref[0]
    tail_parts = split2(cols[:, 4:5] * jnp.exp(cum[Q - 1 : Q, :] - cum))
    step_parts = split2(step)
    b_pair = stacked_left(bc_ref[0])
    d_b = dbc_ref[0, :, :STATE]
    row_x = jnp.zeros((Q, LANES), F32)
    own = slice(EDGE // 2, EDGE // 2 + Q)

    def slope(u):
        sig = sigmoid(u)
        act = u * sig
        return act, sig + act * (1.0 - sig)

    for group in range(INNER // GRP):
        lanes = lanes_of(group)
        d_end = dend_ref[0, 0, :, lanes] + after_ref[0, 0, 0:1, lanes] * pass_ref[
            0, :, lanes
        ].astype(F32)
        tail_wide = spread_heads(tail_parts, table[:, lanes])
        xt = xh_ref[0, :, lanes].astype(F32) + xl_ref[0, :, lanes].astype(F32)
        d_b = d_b + mm3_nt(tail_wide * xt, d_end)
        dxt = dx_ref[0, :, lanes] + tail_wide * mm3_stacked(b_pair, d_end)
        act, grow = slope(u_ref[0, :, lanes])
        ph, plow = split2(dxt * act)
        row_x = row_x + mm(ph, fold_ref[lanes, :]) + mm(plow, fold_ref[lanes, :])
        dy = dyh_ref[0, :, lanes].astype(F32) + dyl_ref[0, :, lanes].astype(F32)
        dx = dxt * spread_heads(step_parts, table[:, lanes]) + skip_ref[:, lanes] * dy
        du_ext[own, lanes] = dx * grow
    _, grow = slope(u_ref[0, :, INNER:])
    d_c = dbc_ref[0, :, STATE:] + dc_ref[0]
    du_ext[own, INNER:] = jnp.concatenate([d_b, d_c], axis=1) * grow

    row_x = row_x[:, :HEADS]
    d_cum = ry_ref[0][:, :HEADS] - step * row_x
    d_decay = sum(
        lax.dot_general(
            tri_ref[...], part, (((0,), (0,)), ((), ())), preferred_element_type=F32
        )
        for part in split3(d_cum)
    )
    d_decay = d_decay + energy[0:1, :HEADS]
    energy[:, :HEADS] = jnp.broadcast_to(d_decay[0:1, :], (8, HEADS))
    d_dt = (row_x + d_decay * neg_a_ref[...]) * sig_ref[0]
    dproj_ref[0, :, CONV_CH:] = d_dt.astype(BF)
    dsmall_ref[0:1, :] += jnp.sum(d_dt, axis=0, keepdims=True)
    dsmall_ref[1:2, :] += jnp.sum(d_decay * step * neg_a_ref[...], axis=0, keepdims=True)

    for group in range(CONV_CH // GRP):
        lanes = lanes_of(group)
        du = du_ext[own, lanes]
        dbias_ref[:, lanes] += jnp.sum(du.reshape(Q // 8, 8, GRP), axis=0)
        taps = [
            jnp.sum((du * ext[EDGE : EDGE + Q, lanes]).reshape(Q // 8, 8, GRP), axis=0)
        ]
        d_in = taps_ref[3:4, lanes] * du
        for ahead in (1, 2, 3):
            before = ext[EDGE - ahead : EDGE - ahead + Q, lanes] * cols[:, ahead - 1 : ahead]
            taps.append(jnp.sum((du * before).reshape(Q // 8, 8, GRP), axis=0))
            later = du_ext[EDGE // 2 + ahead : EDGE // 2 + ahead + Q, lanes]
            d_in = d_in + taps_ref[3 - ahead : 4 - ahead, lanes] * (
                later * cols[:, 5 + ahead : 6 + ahead]
            )
        for place in range(WIDTH):
            dtaps_ref[WIDTH - 1 - place, :, lanes] += taps[place]
        dproj_ref[0, :, lanes] = d_in.astype(BF)

        @pl.when(back == 0)
        def _():
            edge_ref[0, :, lanes] = d_in[Q - 8 :, :]

        @pl.when(back == chunks - 1)
        def _():
            sent = jnp.zeros((8, GRP), F32)
            for ahead in (1, 2, 3):
                sent = sent + taps_ref[3 - ahead : 4 - ahead, lanes] * (
                    du_ext[ahead : ahead + 8, lanes] * edge_cols_ref[0, :, ahead - 1 : ahead]
                )
            rim_grad_ref[0, :, lanes] = sent


def params():
    return pltpu.CompilerParams(
        dimension_semantics=("arbitrary", "arbitrary"), vmem_limit_bytes=VMEM_LIMIT
    )


def fixed(shape):
    return pl.BlockSpec(shape, lambda r, c: (0,) * len(shape))


def tokens(width, last=0):
    return pl.BlockSpec((1, Q, width), lambda r, c: (r, c, last))


def per_row(shape):
    return pl.BlockSpec((1,) + shape, lambda r, c: (r,) + (0,) * len(shape))


def per_chunk(shape):
    return pl.BlockSpec((1, 1) + shape, lambda r, c: (r, c) + (0,) * len(shape))


def flip(spec, chunks):
    inner = spec.index_map
    return pl.BlockSpec(spec.block_shape, lambda r, c: inner(r, chunks - 1 - c))


def before(width):
    per = Q // EDGE
    return pl.BlockSpec((1, EDGE, width), lambda r, c: (r, jnp.maximum(c * per - 1, 0), 0))


def shape_of(dims, kind=F32):
    return jax.ShapeDtypeStruct(dims, kind)


def estimate(flops, moved):
    return pl.CostEstimate(flops=int(flops), bytes_accessed=int(moved), transcendentals=0)


def across():
    return pl.BlockSpec((1, HEADS, Q), lambda r, c: (r, 0, c))


def seg_row():
    return pl.BlockSpec((1, 1, Q), lambda r, c: (r, 0, c))


def front_call(mix, rim, cols, taps, bias, bias_dt, neg_a, table, tri):
    rows, length, _ = mix.shape
    chunks = length // Q
    return pl.pallas_call(
        front_kernel,
        grid=(rows, chunks),
        in_specs=[
            tokens(MIX),
            before(MIX),
            per_row((EDGE, MIX)),
            tokens(16),
            fixed((WIDTH, CONV_CH)),
            fixed((1, CONV_CH)),
            fixed((1, HEADS)),
            fixed((1, HEADS)),
            fixed((HEADS, INNER)),
            fixed((Q, Q)),
        ],
        out_specs=[
            tokens(CONV_CH),
            tokens(INNER),
            tokens(INNER),
            tokens(2 * STATE),
            tokens(HEADS),
            tokens(HEADS),
            tokens(HEADS),
            across(),
            per_chunk((STATE, INNER)),
            per_row((STATE, INNER)),
            per_chunk((8, INNER)),
            per_row((8, INNER)),
        ],
        out_shape=[
            shape_of((rows, length, CONV_CH)),
            shape_of((rows, length, INNER), BF),
            shape_of((rows, length, INNER), BF),
            shape_of((rows, length, 2 * STATE)),
            shape_of((rows, length, HEADS)),
            shape_of((rows, length, HEADS)),
            shape_of((rows, length, HEADS)),
            shape_of((rows, HEADS, length)),
            shape_of((rows, chunks, STATE, INNER)),
            shape_of((rows, STATE, INNER)),
            shape_of((rows, chunks, 8, INNER)),
            shape_of((rows, 8, INNER)),
        ],
        scratch_shapes=[
            pltpu.VMEM((EDGE + Q, CONV_CH), F32),
            pltpu.VMEM((STATE, INNER), F32),
            pltpu.VMEM((8, INNER), F32),
        ],
        compiler_params=params(),
        cost_estimate=estimate(6e9, 30e6),
        name="front",
    )(mix, mix, rim, cols, taps, bias, bias_dt, neg_a, table, tri)


def within_call(bc, cum, cum_t, cols, seg, xh, xl):
    rows, length, _ = xh.shape
    return pl.pallas_call(
        within_kernel,
        grid=(rows, length // Q),
        in_specs=[
            tokens(2 * STATE),
            tokens(HEADS),
            across(),
            tokens(16),
            seg_row(),
            tokens(INNER),
            tokens(INNER),
        ],
        out_specs=tokens(INNER),
        out_shape=shape_of((rows, length, INNER)),
        compiler_params=params(),
        cost_estimate=estimate(8e9, 14e6),
        name="within",
    )(bc, cum, cum_t, cols, seg, xh, xl)


def gate_call(y, u, z, dgn, bc, cum, cols, start, reach, inc, skip, gain, table, fold):
    rows, length, _ = y.shape
    chunks = length // Q
    specs = [
        tokens(INNER),
        tokens(INNER),
        tokens(INNER),
        tokens(INNER),
        tokens(STATE, 1),
        tokens(HEADS),
        tokens(16),
        per_chunk((STATE, INNER)),
        per_chunk((8, INNER)),
        per_row((STATE, INNER)),
        fixed((1, INNER)),
        fixed((1, INNER)),
        fixed((HEADS, INNER)),
        fixed((INNER, LANES)),
    ]
    outs = [
        tokens(INNER),
        tokens(INNER),
        tokens(INNER),
        tokens(INNER),
        tokens(LANES),
        tokens(STATE),
        per_chunk((STATE, INNER)),
        per_row((STATE, INNER)),
        per_chunk((8, INNER)),
        fixed((8, INNER)),
        fixed((8, INNER)),
    ]
    return pl.pallas_call(
        gate_kernel,
        grid=(rows, chunks),
        in_specs=[flip(spec, chunks) for spec in specs],
        out_specs=[flip(spec, chunks) for spec in outs],
        out_shape=[
            shape_of((rows, length, INNER), BF),
            shape_of((rows, length, INNER), BF),
            shape_of((rows, length, INNER), BF),
            shape_of((rows, length, INNER), BF),
            shape_of((rows, length, LANES)),
            shape_of((rows, length, STATE)),
            shape_of((rows, chunks, STATE, INNER)),
            shape_of((rows, STATE, INNER)),
            shape_of((rows, chunks, 8, INNER)),
            shape_of((8, INNER)),
            shape_of((8, INNER)),
        ],
        scratch_shapes=[
            pltpu.VMEM((Q, INNER), F32),
            pltpu.VMEM((Q, INNER), F32),
            pltpu.VMEM((Q, INNER), F32),
            pltpu.VMEM((STATE, INNER), F32),
            pltpu.VMEM((8, INNER), F32),
        ],
        compiler_params=params(),
        cost_estimate=estimate(10e9, 50e6),
        name="gate",
    )(y, u, z, dgn, bc, cum, cols, start, reach, inc, skip, gain, table, fold)


def within_back_call(bc, cum, cum_t, cols, seg, xh, xl, dyh):
    rows, length, _ = xh.shape
    return pl.pallas_call(
        within_back_kernel,
        grid=(rows, length // Q),
        in_specs=[
            tokens(2 * STATE),
            tokens(HEADS),
            across(),
            tokens(16),
            seg_row(),
            tokens(INNER),
            tokens(INNER),
            tokens(INNER),
        ],
        out_specs=[tokens(INNER), tokens(2 * STATE)],
        out_shape=[shape_of((rows, length, INNER)), shape_of((rows, length, 2 * STATE))],
        compiler_params=params(),
        cost_estimate=estimate(12e9, 18e6),
        name="within_back",
    )(bc, cum, cum_t, cols, seg, xh, xl, dyh)


def back_call(
    dx, dbc, dc, u, xh, xl, dyh, dyl, ry, step, cum, sig, cols, edge_cols, bc, dend, after,
    passing, final, whole, inc, mix, rim, taps, skip, neg_a, table, fold, tri,
):
    rows, length, _ = dx.shape
    chunks = length // Q
    specs = [
        tokens(INNER),
        tokens(2 * STATE),
        tokens(STATE),
        tokens(CONV_CH),
        tokens(INNER),
        tokens(INNER),
        tokens(INNER),
        tokens(INNER),
        tokens(LANES),
        tokens(HEADS),
        tokens(HEADS),
        tokens(HEADS),
        tokens(16),
        per_row((8, 8)),
        tokens(STATE),
        per_chunk((STATE, INNER)),
        per_chunk((8, INNER)),
        per_row((STATE, INNER)),
        per_row((STATE, INNER)),
        per_row((8, INNER)),
        per_row((STATE, INNER)),
        tokens(MIX),
        before(MIX),
        per_row((EDGE, MIX)),
        fixed((WIDTH, CONV_CH)),
        fixed((1, INNER)),
        fixed((1, HEADS)),
        fixed((HEADS, INNER)),
        fixed((INNER, LANES)),
        fixed((Q, Q)),
    ]
    outs = [
        tokens(MIX),
        per_row((8, CONV_CH)),
        per_row((8, CONV_CH)),
        fixed((WIDTH, 8, CONV_CH)),
        fixed((8, CONV_CH)),
        fixed((8, HEADS)),
    ]
    return pl.pallas_call(
        back_kernel,
        grid=(rows, chunks),
        in_specs=[flip(spec, chunks) for spec in specs],
        out_specs=[flip(spec, chunks) for spec in outs],
        out_shape=[
            shape_of((rows, length, MIX), BF),
            shape_of((rows, 8, CONV_CH)),
            shape_of((rows, 8, CONV_CH)),
            shape_of((WIDTH, 8, CONV_CH)),
            shape_of((8, CONV_CH)),
            shape_of((8, HEADS)),
        ],
        scratch_shapes=[
            pltpu.VMEM((EDGE + Q, CONV_CH), F32),
            pltpu.VMEM((EDGE + Q, CONV_CH), F32),
            pltpu.VMEM((8, LANES), F32),
        ],
        compiler_params=params(),
        cost_estimate=estimate(10e9, 60e6),
        name="back",
    )(
        dx, dbc, dc, u, xh, xl, dyh, dyl, ry, step, cum, sig, cols, edge_cols, bc, dend, after,
        passing, final, whole, inc, mix, mix, rim, taps, skip, neg_a, table, fold, tri,
    )


def swap_cores(block):
    count = lax.axis_size("rep")
    return lax.ppermute(block, "rep", [(i, (i + 1) % count) for i in range(count)])


def from_shard(block, mask):
    return lax.ppermute(block, "shard", [(i, i ^ mask) for i in range(lax.axis_size("shard"))])


def gather_rows(block):
    count, core, here = lax.axis_size("shard"), lax.axis_index("rep"), lax.axis_index("shard")
    half = block.shape[0] // 2
    mine = lax.dynamic_slice_in_dim(block, core * half, half, 0)
    held = jnp.zeros((count,) + mine.shape, mine.dtype)
    for mask in range(count):
        got = mine if mask == 0 else from_shard(mine, mask)
        held = lax.dynamic_update_index_in_dim(held, got, here ^ mask, 0)
    other = swap_cores(held)
    low = jnp.where(core == 0, held, other)
    high = jnp.where(core == 0, other, held)
    return jnp.stack([low, high], axis=1).reshape((count * 2 * half,) + block.shape[1:])


def reduce_rows(total, narrow):
    count, core, here = lax.axis_size("shard"), lax.axis_index("rep"), lax.axis_index("shard")
    steps, place = lax.axis_size("seq"), lax.axis_index("seq")
    rows = total.shape[0] // count
    half = rows // 2
    kind = BF if narrow else F32
    parts = total.reshape((count, 2, half) + total.shape[1:])
    keep = lax.dynamic_index_in_dim(parts, core, 1, keepdims=False)
    give = lax.dynamic_index_in_dim(parts, 1 - core, 1, keepdims=False)
    held = keep + swap_cores(give)
    mine = lax.dynamic_index_in_dim(held, here, 0, keepdims=False)
    for mask in range(1, count):
        give = lax.dynamic_index_in_dim(held, here ^ mask, 0, keepdims=False)
        mine = mine + from_shard(give.astype(kind), mask).astype(F32)
    pieces = mine.reshape((steps, half // steps) + mine.shape[1:])
    piece = lax.dynamic_index_in_dim(pieces, place, 0, keepdims=False)
    for ahead in range(1, steps):
        route = [(i, (i + ahead) % steps) for i in range(steps)]
        give = lax.dynamic_index_in_dim(pieces, (place + ahead) % steps, 0, keepdims=False)
        piece = piece + lax.ppermute(give, "seq", route)
    out = jnp.zeros_like(pieces)
    out = lax.dynamic_update_index_in_dim(out, piece, place, 0)
    for ahead in range(1, steps):
        route = [(i, (i + ahead) % steps) for i in range(steps)]
        got = lax.ppermute(piece, "seq", route)
        out = lax.dynamic_update_index_in_dim(out, got, (place - ahead) % steps, 0)
    out = out.reshape((half,) + mine.shape[1:])
    other = swap_cores(out)
    low = jnp.where(core == 0, out, other)
    high = jnp.where(core == 0, other, out)
    return jnp.concatenate([low, high], axis=0)


def chain(own, through, direction, kind):
    steps = lax.axis_size("seq")
    result = []
    for row in range(own.shape[0]):
        incoming = jnp.zeros(own.shape[1:], kind)
        for hop in range(steps - 1):
            pair = (hop, hop + 1) if direction > 0 else (steps - 1 - hop, steps - 2 - hop)
            total = through[row] * incoming.astype(F32) + own[row]
            incoming = incoming + lax.ppermute(total.astype(kind), "seq", [pair])
        result.append(incoming)
    return jnp.stack(result)


def token_columns(segment, length):
    rows, whole = segment.shape
    offset = lax.axis_index("seq") * length
    low = jnp.full((rows, 8), -1, jnp.int32)
    high = jnp.full((rows, 8), -2, jnp.int32)
    padded = jnp.concatenate([low, segment, high], axis=1)
    around = lax.dynamic_slice_in_dim(padded, offset, length + 16, 1)
    own = around[:, 8 : 8 + length]
    chunks = length // Q
    start = jnp.repeat(around[:, 7 : 7 + length : Q], Q, axis=1)
    last = jnp.repeat(around[:, 8 + Q - 1 : 8 + length : Q], Q, axis=1)
    ahead = [around[:, 8 + j : 8 + j + length] == own for j in (1, 2, 3)]
    back = [around[:, 8 - j : 8 - j + length] == own for j in (1, 2, 3)]
    masks = back + [own == start, own == last, own] + ahead
    cols = jnp.stack([mask.astype(F32) for mask in masks], axis=-1)
    cols = jnp.pad(cols, ((0, 0), (0, 0), (0, 16 - len(masks))))
    edge = [around[:, j : j + 8] == around[:, :8] for j in (1, 2, 3)]
    edge_cols = jnp.pad(
        jnp.stack([mask.astype(F32) for mask in edge], axis=-1), ((0, 0), (0, 0), (0, 5))
    )
    return cols, edge_cols, own.astype(F32)[:, None, :]


def local(
    hidden,
    segment,
    norm_gain,
    in_weight,
    conv_weight,
    conv_bias,
    dt_bias,
    a_log,
    skip_d,
    inner_gain,
    out_weight,
    cotangent,
):
    rows, length, _ = hidden.shape
    flat = rows * length
    shards = lax.axis_size("shard")
    steps = lax.axis_size("seq")
    forward = [(i, i + 1) for i in range(steps - 1)]
    backward = [(i + 1, i) for i in range(steps - 1)]

    smalls = (norm_gain, conv_weight, conv_bias, dt_bias, a_log, skip_d, inner_gain)
    pack = jnp.concatenate([v.astype(BF).reshape(-1) for v in smalls])
    sizes = [v.size for v in smalls]
    unit = 16 * LANES
    width = -(-pack.size // unit) * unit
    pack = jnp.pad(pack, (0, width - pack.size)).reshape(16, -1)
    pack_all = gather_rows(pack).reshape(shards, width)
    cuts = [sum(sizes[:k]) for k in range(len(sizes) + 1)]
    pieces = [pack_all[:, cuts[k] : cuts[k + 1]].astype(F32) for k in range(len(sizes))]
    gain_n = pieces[0].reshape(-1)
    taps = pieces[1].reshape(shards, WIDTH, -1).transpose(1, 0, 2).reshape(WIDTH, CONV_CH)
    bias = pieces[2].reshape(1, CONV_CH)
    bias_dt = pieces[3].reshape(1, HEADS)
    neg_a = -jnp.exp(pieces[4].reshape(1, HEADS))
    skip = jnp.repeat(pieces[5].reshape(HEADS), HEAD_DIM).reshape(1, INNER)
    gain_i = pieces[6].reshape(1, INNER)
    w_mix = gather_rows(in_weight[:, INNER:].astype(BF))
    w_z = gather_rows(in_weight[:, :INNER].astype(BF))
    w_out = gather_rows(out_weight.astype(BF))

    head_of = jnp.arange(INNER) // HEAD_DIM
    table = (jnp.arange(HEADS)[:, None] == head_of[None, :]).astype(BF)
    fold = (head_of[:, None] == jnp.arange(LANES)[None, :]).astype(BF)
    tri = (jnp.arange(Q)[:, None] >= jnp.arange(Q)[None, :]).astype(BF)

    cols, edge_cols, seg = token_columns(segment, length)

    def front_norm(block):
        mean_sq = jnp.mean(block * block, axis=-1, keepdims=True)
        return block * lax.rsqrt(mean_sq + norm_epsilon)

    rim_hidden = lax.ppermute(hidden[:, length - EDGE :, :], "seq", forward)
    hidden_f = hidden.astype(F32)
    normed = (front_norm(hidden_f) * gain_n).astype(BF).reshape(flat, D)
    rim_normed = (front_norm(rim_hidden.astype(F32)) * gain_n).astype(BF).reshape(-1, D)
    mix = mm(normed, w_mix).astype(BF).reshape(rows, length, MIX)
    rim = mm(rim_normed, w_mix).astype(BF).reshape(rows, EDGE, MIX)

    u, xh, xl, bc, step, cum, sig, cum_t, start, final, reach, whole = front_call(
        mix, rim, cols, taps, bias, bias_dt, neg_a, table, tri
    )
    incoming = chain(final, whole[:, 0:1, :], 1, BF)
    y = within_call(bc, cum, cum_t, cols, seg, xh, xl)
    z = mm(normed, w_z).astype(BF).reshape(rows, length, INNER)
    cot_flat = cotangent.reshape(flat, D)
    dgn = mm_nt(cot_flat, w_out).reshape(rows, length, INNER)

    (gnorm, dz, dyh, dyl, ry, dc, dend, dstart, after, dskip, dgain) = gate_call(
        y, u, z, dgn, bc, cum, cols, start, reach, incoming, skip, gain_i, table, fold
    )
    passing = chain(dstart, whole[:, 0:1, :], -1, BF)
    dx, dbc = within_back_call(bc, cum, cum_t, cols, seg, xh, xl, dyh)
    gnorm_flat = gnorm.reshape(flat, INNER)
    branch = mm(gnorm_flat, w_out).reshape(rows, length, D)
    result = (hidden_f + branch).astype(BF)

    def weight_grad(left, right):
        return lax.dot_general(left, right, (((0,), (0,)), ((), ())), preferred_element_type=F32)

    grad_wout = reduce_rows(weight_grad(gnorm_flat, cot_flat), True)
    dz_flat = dz.reshape(flat, INNER)
    grad_wz = reduce_rows(weight_grad(normed, dz_flat), True)
    dnormed_z = mm_nt(dz_flat, w_z)

    dmix, edge, rim_grad, dtaps, dbias, dsmall = back_call(
        dx, dbc, dc, u, xh, xl, dyh, dyl, ry, step, cum, sig, cols, edge_cols, bc, dend, after,
        passing, final, whole, incoming, mix, rim, taps, skip, neg_a, table, fold, tri,
    )
    back_rim = lax.ppermute(rim_grad.astype(BF), "seq", backward).astype(F32)
    fixed_edge = (edge + back_rim).astype(BF)
    dmix = lax.dynamic_update_slice(dmix, fixed_edge, (0, length - 8, 0))
    dmix = dmix.reshape(flat, MIX)
    grad_wmix = reduce_rows(weight_grad(normed, dmix), True)
    dnormed = (dnormed_z + mm_nt(dmix, w_mix)).reshape(rows, length, D)

    inverse = lax.rsqrt(jnp.mean(hidden_f * hidden_f, axis=-1, keepdims=True) + norm_epsilon)
    unit_h = hidden_f * inverse
    grad_gain = jnp.sum(dnormed * unit_h, axis=(0, 1))
    scaled = dnormed * gain_n
    along = jnp.mean(scaled * unit_h, axis=-1, keepdims=True)
    hidden_grad = cotangent.astype(F32) + inverse * (scaled - unit_h * along)

    small_grads = (
        grad_gain,
        jnp.sum(dtaps, axis=1),
        jnp.sum(dbias, axis=0),
        dsmall[0],
        dsmall[1],
        jnp.sum(dskip.reshape(8, HEADS, HEAD_DIM), axis=(0, 2)),
        jnp.sum(dgain, axis=0),
    )
    by_shard = [
        g.reshape(WIDTH, shards, -1).transpose(1, 0, 2).reshape(shards, -1)
        if g.ndim == 2
        else g.reshape(shards, -1)
        for g in small_grads
    ]
    packed = jnp.concatenate(by_shard, axis=1)
    grid = 2 * steps * LANES
    padded = -(-packed.shape[1] // grid) * grid
    packed = jnp.pad(packed, ((0, 0), (0, padded - packed.shape[1])))
    packed = packed.reshape(shards * 2 * steps, -1)
    small_sum = reduce_rows(packed, False).reshape(-1)
    ends = [sum(g.shape[1] for g in by_shard[:k]) for k in range(len(by_shard) + 1)]
    parts = [small_sum[ends[k] : ends[k + 1]] for k in range(len(by_shard))]
    return (
        result,
        hidden_grad,
        parts[0],
        jnp.concatenate([grad_wz, grad_wmix], axis=1),
        parts[1].reshape(WIDTH, -1),
        parts[2],
        parts[3],
        parts[4],
        parts[5],
        parts[6],
        grad_wout,
    )


def solution(mesh):
    tokens_spec = P(("rep", "shard"), "seq", None)
    small = P("shard")
    in_specs = (
        tokens_spec,
        P(("rep", "shard"), None),
        small,
        P("shard", None),
        P(None, "shard"),
        small,
        small,
        small,
        small,
        small,
        P("shard", None),
        tokens_spec,
    )
    out_specs = (
        tokens_spec,
        tokens_spec,
        small,
        P("shard", None),
        P(None, "shard"),
        small,
        small,
        small,
        small,
        small,
        P("shard", None),
    )
    return jax.shard_map(local, mesh=mesh, in_specs=in_specs, out_specs=out_specs, check_vma=False)
```
